256 devices in a mesh: ctx: 32 (over x, z), head: 8 (over y, core).
Axes of the slice: x: 4, y: 4, z: 8, core: 2. Of those that a mesh axis runs over, the one named last changes fastest.
Arguments:
- hidden_states: bfloat16 [16384, 8192], P('ctx', 'head'), may hold values from -48 to 48
- w_query: bfloat16 [8192, 8192], P('ctx', 'head'), may hold values from -0.25 to 0.25
- w_key: bfloat16 [8192, 1024], P('ctx', 'head'), may hold values from -0.25 to 0.25
- thresholds: int32 [8, 8], P('head'), may hold values from 1 to 16
Outputs:
- row_mass: float32 [8, 8, 2048, 16], P('head', None, 'ctx')
- block_mass: float32 [8, 8, 16, 16], P('head')
- coverage: float32 [8, 8, 16], P('head')
The draws below stay inside these ranges and needn't reach their ends.
All inputs are finite; a program needn't handle non-finite values.
Results may differ from the reference program's by a relative error of at most 0.0035.
Values may be sent and summed in bfloat16 or wider, within the bound.
No kernel may reach another device: no remote copies, remote signals or barrier semaphores. Data moves between devices by JAX's collectives and lax.ppermute only.
A program may use at most 128 MiB of HBM per device.

```python
import math
import jax
import jax.numpy as jnp
from jax import lax

D = 8192
HD = 128
QH = 8
STRIDE = 8
BLOCK = 1024
GROUPS = 8
TOKENS = 16384
RROWS = 2048
NB = 16


def common_part(key):
    return jax.random.normal(key, (D, HD), jnp.float32) / math.sqrt(D)


def draw_w_query(key, part):
    shared = common_part(key)
    key = jax.random.fold_in(key, 11)
    own_part = jax.random.normal(key, (D, GROUPS * QH * HD), jnp.float32) / math.sqrt(D)
    total = own_part + jnp.tile(shared, (1, GROUPS * QH))
    return jnp.clip(total, -0.25, 0.25).astype(jnp.bfloat16)


def draw_w_key(key, part):
    shared = common_part(key)
    key = jax.random.fold_in(key, 23)
    own_part = jax.random.normal(key, (D, GROUPS * HD), jnp.float32) / math.sqrt(D)
    total = own_part + jnp.tile(shared, (1, GROUPS))
    return jnp.clip(total, -0.25, 0.25).astype(jnp.bfloat16)


def draw_hidden_states(key, part):
    key = jax.random.fold_in(key, 31)
    key_noise, key_dir, key_amp = jax.random.split(key, 3)
    group_count = TOKENS // STRIDE
    pair_count = group_count // 2
    amplitude = jax.random.uniform(key_amp, (pair_count, 2), jnp.float32, 0.0, 2.0)
    noise = jax.random.normal(key_noise, (TOKENS, D), jnp.float32)
    direction = jax.random.normal(key_dir, (pair_count, D), jnp.float32)
    shared_rows = jnp.repeat(direction, 2 * STRIDE, axis=0) * jnp.repeat(amplitude.reshape(group_count), STRIDE)[:, None]
    return jnp.clip(noise + shared_rows, -48.0, 48.0).astype(jnp.bfloat16)


def set_ends(array, stream_key, smallest, high):
    shape = array.shape
    index_at = [jax.random.randint(jax.random.fold_in(stream_key, axis), (), 0, shape[axis]) for axis in range(len(shape))]
    array = array.at[tuple(index_at)].set(smallest)
    longest = shape.index(max(shape))
    index_at[longest] = (index_at[longest] + 1) % shape[longest]
    return array.at[tuple(index_at)].set(high)


def setup_inputs(seed: int = 0) -> dict:
    key_list = jax.random.split(jax.random.key(seed), 5)
    return {
        "hidden_states": draw_hidden_states(jax.random.fold_in(key_list[4], 71), 0),
        "w_query": draw_w_query(jax.random.fold_in(key_list[4], 71), 0),
        "w_key": draw_w_key(jax.random.fold_in(key_list[4], 71), 0),
        "thresholds": set_ends(jax.random.randint(key_list[3], (GROUPS, QH), 1, NB + 1), jax.random.fold_in(key_list[3], 1), 1, NB).astype(jnp.int32),
    }


def dense_mass(query_rows, positions, key_block, score_scale, block_rows):
    scores = jnp.dot(query_rows, key_block.T, preferred_element_type=jnp.float32) * score_scale
    key_index = jnp.arange(key_block.shape[0], dtype=jnp.int32)
    allowed = key_index[None, :] <= positions[:, None]
    scores = jnp.where(allowed, scores, -jnp.inf)
    top_score = lax.optimization_barrier(jnp.max(scores, axis=1, keepdims=True))
    expo_terms = jnp.where(allowed, jnp.exp(scores - top_score), 0.0)
    probabilities = expo_terms / lax.optimization_barrier(jnp.sum(expo_terms, axis=1, keepdims=True))
    return probabilities.reshape(probabilities.shape[0], key_block.shape[0] // block_rows, block_rows).sum(axis=2)

def reference(hidden_states, w_query, w_key, thresholds):
    block_rows = BLOCK // STRIDE
    q_proj = jnp.dot(hidden_states, w_query, preferred_element_type=jnp.float32).astype(jnp.bfloat16)
    k_proj = jnp.dot(hidden_states, w_key, preferred_element_type=jnp.float32).astype(jnp.bfloat16)
    query_rev = q_proj.reshape(RROWS, STRIDE, GROUPS, QH, HD)[:, ::-1]
    query_rev = query_rev.transpose(2, 3, 0, 1, 4).reshape(GROUPS * QH, RROWS, STRIDE * HD)
    key_groups = k_proj.reshape(RROWS, STRIDE, GROUPS, HD).transpose(2, 0, 1, 3).reshape(GROUPS, RROWS, STRIDE * HD)
    key_each = jnp.repeat(key_groups, QH, axis=0)
    positions = jnp.arange(RROWS, dtype=jnp.int32)
    score_scale = 1.0 / (math.sqrt(HD) * STRIDE)

    def per_head(paired):
        return dense_mass(paired[0], positions, paired[1], score_scale, block_rows)
    row_mass = lax.map(per_head, (query_rev, key_each))
    block_mass = row_mass.reshape(GROUPS * QH, NB, block_rows, NB).sum(axis=2) / block_rows
    ordered = -jnp.sort(-block_mass, axis=2)
    kept_ranks = jnp.arange(NB, dtype=jnp.int32)[None, None, :] < thresholds.reshape(GROUPS * QH)[:, None, None]
    coverage = lax.optimization_barrier(jnp.sum(jnp.where(kept_ranks, ordered, 0.0), axis=2))
    return (row_mass.reshape(GROUPS, QH, RROWS, NB), block_mass.reshape(GROUPS, QH, NB, NB), coverage.reshape(GROUPS, QH, NB))
```

```python
import math

import jax
import jax.numpy as jnp
from jax import lax
from jax.sharding import Mesh
from jax.sharding import PartitionSpec as P

NX, NZ, NY, NC = 4, 8, 4, 2
STRIDE = 8
HD = 128
QH = 8
PAIR = 2
BLOCK_ROWS = 128
NB = 16
F32 = jnp.float32
BF16 = jnp.bfloat16


def shift(a, axis, step, size):
    return lax.ppermute(a, axis, [(i, (i + step) % size) for i in range(size)])


def spread(a, turn):
    pairs = [(x * NY + y, ((y + turn) % NX) * NY + x) for x in range(NX) for y in range(NY)]
    return lax.ppermute(a, ("x", "y"), pairs)


def swap_xy(a):
    return lax.ppermute(
        a, ("x", "y"), [(x * NY + y, y * NY + x) for x in range(NX) for y in range(NY)]
    )


def pick(a, index, axis=0):
    return lax.dynamic_index_in_dim(a, index, axis, keepdims=False)


def both_cores(a):
    other = shift(a, "c", 1, NC)
    first = lax.axis_index("c") == 0
    return jnp.where(first, a, other), jnp.where(first, other, a)


def body(hidden, w_query, w_key, thresholds):
    x, y, z = lax.axis_index("x"), lax.axis_index("y"), lax.axis_index("z")
    tokens = hidden.shape[0]
    rows = tokens // STRIDE
    depth = w_query.shape[0]
    scale = 1.0 / (math.sqrt(HD) * STRIDE)

    pieces = []
    for turn in range(NX):
        k = (y + turn) % NX
        piece = lax.dynamic_slice(w_query, (0, k * PAIR * HD), (depth, PAIR * HD))
        pieces.append(spread(piece, turn))
    pieces = jnp.stack(pieces)
    w_mine = jnp.concatenate([pick(pieces, (x - g) % NX) for g in range(NY)], axis=1)
    w_full = lax.all_gather(w_mine, "z", axis=0, tiled=True)

    wk_mine = swap_xy(w_key)
    wk_full = lax.all_to_all(
        jnp.broadcast_to(wk_mine[None], (NZ,) + wk_mine.shape), "z", 0, 0, tiled=True
    ).reshape(NZ * depth, HD)

    chunks = [hidden] + [shift(hidden, "x", s, NX) for s in range(1, NX)]
    wide = [jnp.concatenate(both_cores(c), axis=1) for c in chunks]

    k_parts = jnp.stack(
        [jnp.dot(c, wk_full, preferred_element_type=F32).astype(F32) for c in wide]
    )
    k_sum = 0.0
    for turn in range(NX):
        k_sum = k_sum + spread(pick(k_parts, (x - y - turn) % NX), turn)
    k_rows = k_sum.astype(BF16).reshape(rows, STRIDE, HD)[:, ::-1].reshape(rows, STRIDE * HD)
    k_row = [k_rows] + [shift(k_rows, "x", s, NX) for s in range(1, NX)]
    k_row = jnp.stack(k_row)
    k_row = jnp.concatenate([pick(k_row, (x - g) % NX) for g in range(NX)], axis=0)
    keys = lax.all_gather(k_row, "z", axis=0, tiled=True)

    all_x = jnp.concatenate(wide, axis=0)
    partial = jnp.stack(
        [
            jnp.dot(all_x, w_full[:, g * PAIR * HD : (g + 1) * PAIR * HD], preferred_element_type=F32)
            .astype(BF16)
            for g in range(NY)
        ]
    )
    parts = lax.all_to_all(partial, "y", 0, 0, tiled=True)
    q = jnp.sum(parts.astype(F32), axis=0).astype(BF16)
    q = q.reshape(NX * rows, STRIDE, PAIR, HD).transpose(2, 0, 1, 3)
    q = q.reshape(PAIR * NX * rows, STRIDE * HD)

    scores = jnp.einsum("kw,rw->kr", keys, q, preferred_element_type=F32) * scale
    row = jnp.arange(rows, dtype=jnp.int32)
    zs = jnp.arange(NZ, dtype=jnp.int32)
    xs = jnp.arange(NX, dtype=jnp.int32)
    key_pos = ((xs[None, :] * NZ + zs[:, None]) * rows)[:, :, None] + row
    key_pos = key_pos.reshape(-1)
    q_pos = ((((x - xs) % NX) * NZ + z) * rows)[:, None] + row
    q_pos = jnp.broadcast_to(q_pos[None], (PAIR, NX, rows)).reshape(-1)
    allowed = key_pos[:, None] <= q_pos[None, :]
    scores = jnp.where(allowed, scores, -jnp.inf)
    top = jnp.max(scores, axis=0, keepdims=True)
    terms = jnp.exp(scores - top)
    half = terms.reshape(NZ // 2, 2, NX, rows, -1).sum(axis=(1, 3))
    mass = half.transpose(1, 0, 2).reshape(NB, -1)
    mass = mass / jnp.sum(mass, axis=0, keepdims=True)
    mass = mass.reshape(NB, PAIR, NX, rows)

    back = [shift(mass[:, :, s], "x", -s, NX) if s else mass[:, :, 0] for s in range(NX)]
    back = jnp.stack(back)
    row_mass = jnp.stack([pick(back, (p - x) % NX) for p in range(NX)])
    row_mass = row_mass.transpose(0, 2, 3, 1).reshape(1, QH, rows, NB)

    part = mass.sum(axis=3) / BLOCK_ROWS
    part = jnp.stack([pick(part, (x - g) % NX, 2) for g in range(NX)])
    part = part.reshape(1, NX * NB * PAIR)
    every = lax.all_to_all(
        jnp.broadcast_to(part, (NX * NZ, part.shape[1])), ("x", "z"), 0, 0, tiled=True
    )
    every = every.reshape(NX, NZ // 2, 2, NX, NB, PAIR).sum(axis=2)
    block_mass = every.transpose(0, 4, 2, 1, 3).reshape(QH, NB, NB)
    mine = block_mass[:, :, :, None]
    others = block_mass[:, :, None, :]
    at = jnp.arange(NB, dtype=jnp.int32)
    ahead = (others > mine) | ((others == mine) & (at[None, :] < at[:, None]))
    rank = jnp.sum(ahead.astype(jnp.int32), axis=3)
    coverage = jnp.sum(jnp.where(rank < thresholds[0][:, None, None], block_mass, 0.0), axis=2)
    return row_mass, block_mass[None], coverage[None]


def solution(mesh):
    split = Mesh(mesh.devices.reshape(NX, NZ, NY, NC), ("x", "z", "y", "c"))
    ctx, head = ("x", "z"), ("y", "c")
    return jax.shard_map(
        body,
        mesh=split,
        in_specs=(P(ctx, head), P(ctx, head), P(ctx, head), P(head, None)),
        out_specs=(P(head, None, ctx, None), P(head, None, None, None), P(head, None, None)),
        check_vma=False,
    )
```
